128 devices in a mesh: elec: 8 (over x_hi, y), space: 16 (over z, x_lo, core).
Axes of the slice: x: 4 (x_hi: 2, x_lo: 2; x = x_hi * 2 + x_lo), y: 4, z: 4, core: 2. Of those that a mesh axis runs over, the one named last changes fastest.
Arguments:
- potentials: float32 [32, 1024, 8192], P('space', 'elec'), may hold values from -6 to 6
- measurements: int32 [16384, 4], replicated, may hold values from 0 to 1023, all different within a row
- residuals: float32 [2, 16384], replicated, may hold values from -0.03 to 0.03
- conductivity: float32 [32, 8192], P('space', 'elec'), may hold values from 0.1 to 1
- inside: int32 [32, 8192], P('space', 'elec'), may hold values 0 or 1
Outputs:
- gradient: float32 [2, 32, 8192], P(None, 'space', 'elec')
- scaled: float32 [2, 32, 8192], P(None, 'space', 'elec')
The draws below stay inside these ranges and needn't reach their ends.
Inputs may be any that keep to these rules, and one draw needn't show every extreme that they name: `measurements`: each row names four different electrodes, in the order A, B, M, N.
All inputs are finite; a program needn't handle non-finite values. No bound on the sum of `inside` on one device may be relied on, other than what follows from the above.
Results may differ from the reference program's by a relative error of at most 0.0066.
Values may be sent and summed in bfloat16 or wider, within the bound.
A program may use at most 256 MiB of HBM per device.

```python
import math
import jax
import jax.numpy as jnp
from jax import lax

ELECTRODE_COUNT = 1024
QUADRIPOLE_COUNT = 16384
LAPSE_FRAMES = 2
NY = 128
NX = 64
NZ = 32


def place_ends(result, rng, least, top_value):
    dims = result.shape
    spot = [jax.random.randint(jax.random.fold_in(rng, axis), (), 0, dims[axis]) for axis in range(len(dims))]
    result = result.at[tuple(spot)].set(least)
    longest = dims.index(max(dims))
    spot[longest] = (spot[longest] + 1) % dims[longest]
    return result.at[tuple(spot)].set(top_value)


def block_scale(own_key, extent, pieces, smallest, top_value):
    def one(dim, parts):
        steps = jax.random.uniform(jax.random.fold_in(jax.random.fold_in(own_key, 6), dim), (parts,), jnp.float32, smallest / len(pieces), top_value / len(pieces))
        return jnp.repeat(jnp.exp(steps), extent[dim] // parts).reshape((-1,) + (1,) * (len(extent) - dim - 1))

    loudness = one(*pieces[0])
    for cut in pieces[1:]:
        loudness = loudness * one(*cut)
    return loudness


def different_ones(own_key, rows, count, top, lift):
    ranking = jax.random.permutation(jax.random.fold_in(own_key, 1), count)
    boost = ranking
    for power in range(3):
        boost = boost * boost // count
    boost = boost * lift // count
    tickets = jax.random.randint(jax.random.fold_in(own_key, 2), (rows, count), 0, 4096) + boost
    holders = jax.random.permutation(jax.random.fold_in(own_key, 3), rows)[jnp.arange(count) % rows]
    tickets = jnp.where(jnp.arange(rows)[:, None] == holders[None, :], 1 << 14, tickets)
    score = tickets * count + jnp.arange(count)
    return lax.top_k(score.astype(jnp.int32), top)[1].astype(jnp.int32)


def scatter_about(own_key, dims, deviation, reach, cuts=(), held_as=jnp.bfloat16):
    entries = deviation * jax.random.normal(own_key, dims, jnp.float32)
    if cuts:
        entries = entries * block_scale(own_key, dims, cuts, -0.22, 0.18)
    return jnp.clip(entries, -reach, reach).astype(held_as)


def setup_inputs(seed: int = 0) -> dict:
    key_list = jax.random.split(jax.random.key(seed), 6)
    return {
        "potentials": scatter_about(key_list[0], (NZ, ELECTRODE_COUNT, NX * NY), 1.0, 6.0, ((0, 16), (1, 8)), jnp.float32),
        "measurements": different_ones(key_list[1], QUADRIPOLE_COUNT, ELECTRODE_COUNT, 4, 0),
        "residuals": scatter_about(key_list[2], (LAPSE_FRAMES, QUADRIPOLE_COUNT), 0.005, 0.03, (), jnp.float32),
        "conductivity": jnp.clip(jnp.exp(math.log(1.0) - 2.3025851 * jax.random.uniform(key_list[3], (NZ, NX * NY), jnp.float32) ** block_scale(key_list[3], (NZ, NX * NY), ((0, 16), (1, 8)), -0.2, 0.2)), 0.1, 1.0),
        "inside": place_ends((jax.random.randint(key_list[4], (NZ, NX * NY), 0, 4) < 3).astype(jnp.int32), jax.random.fold_in(key_list[4], 1), 0, 1),
    }


def adjoint_weights(measurements, residuals):
    frames = residuals.shape[0]
    src_a = measurements[:, 0]
    src_b = measurements[:, 1]
    pot_m = measurements[:, 2]
    pot_n = measurements[:, 3]
    offset = (jnp.arange(frames, dtype=jnp.int32) * (ELECTRODE_COUNT * ELECTRODE_COUNT))[:, None]
    index = jnp.concatenate([offset + pot_m * ELECTRODE_COUNT + src_a, offset + pot_n * ELECTRODE_COUNT + src_a, offset + pot_m * ELECTRODE_COUNT + src_b, offset + pot_n * ELECTRODE_COUNT + src_b], axis=1).astype(jnp.int32)
    value_entries = jnp.concatenate([residuals, -residuals, -residuals, residuals], axis=1).astype(jnp.float32)
    flat = jax.ops.segment_sum(value_entries.reshape(-1), index.reshape(-1), num_segments=frames * ELECTRODE_COUNT * ELECTRODE_COUNT)
    return flat.reshape(frames * ELECTRODE_COUNT, ELECTRODE_COUNT).astype(jnp.bfloat16)

def forward_diff(grid, along):
    change = jnp.diff(grid, axis=along)
    return jnp.concatenate([change, jnp.zeros_like(lax.slice_in_dim(grid, 0, 1, axis=along))], axis=along)

def reference(potentials, measurements, residuals, conductivity, inside):
    frames = residuals.shape[0]
    weights = adjoint_weights(measurements, residuals)
    field = potentials.astype(jnp.bfloat16)

    def adjoint_plane(plane):
        return jnp.dot(weights, plane, preferred_element_type=jnp.float32).astype(jnp.bfloat16).reshape(frames, ELECTRODE_COUNT, NX * NY)

    def planar(plane, adjoint):
        grid = plane.astype(jnp.float32).reshape(1, ELECTRODE_COUNT, NX, NY)
        agrid = adjoint.astype(jnp.float32).reshape(frames, ELECTRODE_COUNT, NX, NY)
        total = jnp.zeros((frames, NX, NY), jnp.float32)
        for along in (2, 3):
            total = total + lax.optimization_barrier(jnp.sum(forward_diff(grid, along) * forward_diff(agrid, along), axis=1))
        return total.reshape(frames, NX * NY)

    def step(carry, plane):
        upper, upper_adjoint = carry
        adjoint = adjoint_plane(plane)
        depth_u = upper.astype(jnp.float32) - plane.astype(jnp.float32)
        depth_v = upper_adjoint.astype(jnp.float32) - adjoint.astype(jnp.float32)
        sens = planar(plane, adjoint) + lax.optimization_barrier(jnp.sum(depth_u[None] * depth_v, axis=1))
        return ((plane, adjoint), sens)
    init = (field[NZ - 1], adjoint_plane(field[NZ - 1]))
    unused, sens = lax.scan(step, init, field, reverse=True)
    cell_sensitivity = jnp.transpose(sens, (1, 0, 2))
    gradient = -(conductivity * inside.astype(jnp.float32))[None] * cell_sensitivity
    depth = jnp.arange(NZ, dtype=jnp.float32)
    weight = 1.0 + 2.0 * depth / NZ
    coverage = jnp.cumsum(weight[None, :, None] * gradient * gradient, axis=1)
    scaled = gradient / jnp.sqrt(1.0 + coverage / (depth + 1.0)[None, :, None])
    return (gradient, scaled)
```

```python
import functools

import jax
import jax.numpy as jnp
from jax import lax
from jax.experimental import pallas as pl
from jax.experimental.pallas import tpu as pltpu
from jax.sharding import PartitionSpec as P

ELECTRODES = 1024
NY = 128
ROWS = 4
SLAB = (ROWS + 1) * NY
OWN = ROWS * NY
MESH = pl.DeviceIdType.MESH
BF = jnp.bfloat16
F32 = jnp.float32
OFFSETS = [(2, 2), (1, 0), (0, 3), (2, 1), (3, 0), (0, 1), (1, 2), (3, 3), (2, 0), (0, 2), (1, 1), (3, 2), (2, 3), (1, 3), (3, 1)]
QUAD_CHUNK = 1024
ZCOL = 4 * SLAB


def device_of(x, y, z, c):
    return (lax.div(x, 2) * 4 + y, z * 4 + lax.rem(x, 2) * 2 + c)


def kernel_body(pot, quads, resid, cond, inside, grad_out, scaled_out,
                stage, send, field, weights, wacc, psi, sens, mine, other, totals,
                stage_sem, own_sem, out_sem, in_sem, zs_sem, zr_sem, ws_sem, wr_sem, ds_sem, dr_sem,
                ps_sem, pr_sem, ts_sem, tr_sem):
    e = lax.axis_index("elec")
    s = lax.axis_index("space")
    y = lax.rem(e, 4)
    xh = lax.div(e, 4)
    c = lax.rem(s, 2)
    xl = lax.rem(lax.div(s, 2), 2)
    z = lax.div(s, 4)
    x = xh * 2 + xl
    n_off = len(OFFSETS)

    cells = pot.shape[2]
    quarter = cells // 4

    def stage_copy(p, q):
        cols = pl.ds(q * quarter, quarter)
        return pltpu.make_async_copy(pot.at[p, :, cols], stage.at[p, :, cols], stage_sem.at[p, q])

    for p in range(2):
        for q in range(4):
            stage_copy(p, q).start()

    bar = pltpu.get_barrier_semaphore()
    for dx, dy in OFFSETS:
        pl.semaphore_signal(bar, inc=1, device_id=device_of(lax.rem(x + dx, 4), lax.rem(y + dy, 4), z, c), device_id_type=MESH)
    for i in range(1, 16):
        pl.semaphore_signal(bar, inc=1, device_id=(e, lax.rem(s + i, 16)), device_id_type=MESH)

    def slab_copy(p, i):
        dx, dy = OFFSETS[i]
        tx = lax.rem(x + dx, 4)
        ty = lax.rem(y + dy, 4)
        block = (lax.div(tx, 2) * 4 + ty) * 2 + lax.rem(tx, 2)
        return pltpu.make_async_remote_copy(
            src_ref=send.at[p, :, pl.ds(pl.multiple_of(block * OWN, OWN), SLAB)],
            dst_ref=field.at[pl.ds(pl.multiple_of(e * 128, 128), 128), pl.ds(pl.multiple_of((xl * 2 + p) * SLAB, 128), SLAB)],
            send_sem=out_sem.at[p, i], recv_sem=in_sem.at[p, i],
            device_id=device_of(tx, ty, z, c), device_id_type=MESH)

    row_block = e * 2 + xl

    def own_copy(p):
        return pltpu.make_async_copy(
            send.at[p, :, pl.ds(pl.multiple_of(row_block * OWN, OWN), SLAB)],
            field.at[pl.ds(pl.multiple_of(e * 128, 128), 128), pl.ds(pl.multiple_of((xl * 2 + p) * SLAB, 128), SLAB)],
            own_sem.at[p])

    for p in range(2):
        send[p, :, pl.ds(cells, NY)] = jnp.zeros((128, NY), BF)
        for q in range(4):
            stage_copy(p, q).wait()

            def cast(i, _):
                rows = pl.ds(pl.multiple_of(i * 16, 16), 16)
                cols = pl.ds(q * quarter, quarter)
                send[p, rows, cols] = stage[p, rows, cols].astype(BF)
                return 0
            lax.fori_loop(0, 8, cast, 0)
        if p == 0:
            pl.semaphore_wait(bar, n_off + 15)
        for i in range(n_off):
            slab_copy(p, i).start()
        own_copy(p).start()

    quarter_f = 256
    half_e = 512
    wacc[...] = jnp.zeros_like(wacc)
    f_ids = z * quarter_f + lax.broadcasted_iota(jnp.int32, (quarter_f, QUAD_CHUNK), 0)
    e_ids = c * half_e + lax.broadcasted_iota(jnp.int32, (half_e, QUAD_CHUNK), 0)

    def add_quads(i, _):
        cols = pl.ds(pl.multiple_of(i * QUAD_CHUNK, QUAD_CHUNK), QUAD_CHUNK)
        left = (jnp.where(quads[2:3, cols] == f_ids, 1.0, 0.0) - jnp.where(quads[3:4, cols] == f_ids, 1.0, 0.0)).astype(BF)
        right = (jnp.where(quads[0:1, cols] == e_ids, 1.0, 0.0) - jnp.where(quads[1:2, cols] == e_ids, 1.0, 0.0)).astype(BF)
        for k in range(2):
            r = resid[k:k + 1, cols]
            hi = r.astype(BF)
            lo = (r - hi.astype(F32)).astype(BF)
            for part in (hi, lo):
                wacc[k] += lax.dot_general(left * part, right, (((1,), (1,)), ((), ())), preferred_element_type=F32)
        return 0
    lax.fori_loop(0, quads.shape[1] // QUAD_CHUNK, add_quads, 0)

    def block_of(zz, cc):
        return weights.at[:, pl.ds(pl.multiple_of(zz * quarter_f, quarter_f), quarter_f), pl.ds(pl.multiple_of(cc * half_e, half_e), half_e)]

    weights[:, pl.ds(pl.multiple_of(z * quarter_f, quarter_f), quarter_f), pl.ds(pl.multiple_of(c * half_e, half_e), half_e)] = wacc[...].astype(BF)

    def w_copy(d):
        tz = lax.rem(z + d, 4)
        return pltpu.make_async_remote_copy(
            src_ref=block_of(z, c), dst_ref=block_of(z, c), send_sem=ws_sem.at[d], recv_sem=wr_sem.at[d],
            device_id=device_of(x, y, tz, c), device_id_type=MESH)

    def w_across(d):
        zz = lax.rem(z + 4 - d, 4)
        return pltpu.make_async_remote_copy(
            src_ref=block_of(zz, c), dst_ref=block_of(zz, c), send_sem=ds_sem.at[d], recv_sem=dr_sem.at[d],
            device_id=device_of(x, y, z, 1 - c), device_id_type=MESH)

    for d in (1, 3, 2):
        w_copy(d).start()
    w_across(0).start()

    for i in range(n_off):
        slab_copy(0, i).wait_recv()
    own_copy(0).wait()

    def halo_copy(j):
        slot = jnp.where(c == 0, 2 - 2 * j, 2 * j)
        if j == 0:
            target = device_of(x, y, z, 1 - c)
        else:
            target = device_of(x, y, jnp.where(c == 0, lax.rem(z + 3, 4), z), 1 - c)
        return pltpu.make_async_remote_copy(
            src_ref=field.at[:, pl.ds(pl.multiple_of(slot * SLAB, 128), OWN)],
            dst_ref=field.at[:, pl.ds(ZCOL + j * OWN, OWN)],
            send_sem=zs_sem.at[j], recv_sem=zr_sem.at[j], device_id=target, device_id_type=MESH)

    for j in (1, 0):
        halo_copy(j).start()

    for d in (1, 3, 2):
        w_copy(d).wait_recv()
        w_across(d).start()
    for d in (0, 1, 3, 2):
        w_across(d).wait_recv()

    def adjoint(col, width):
        def block(i, _):
            k = lax.div(i, 4)
            rows = pl.ds(pl.multiple_of(lax.rem(i, 4) * 256, 256), 256)
            cols = pl.ds(col, width)
            psi[k, rows, cols] = jnp.dot(weights[k, rows, :], field[:, cols], preferred_element_type=F32).astype(BF)
            return 0
        lax.fori_loop(0, 8, block, 0)

    adjoint(0, SLAB)
    adjoint(2 * SLAB, SLAB)

    for j in range(2):
        halo_copy(j).wait_recv()
        adjoint(ZCOL + j * OWN, OWN)

    for i in range(n_off):
        slab_copy(1, i).wait_recv()
    own_copy(1).wait()
    adjoint(SLAB, SLAB)
    adjoint(3 * SLAB, SLAB)

    lane_keep = (lax.broadcasted_iota(jnp.int32, (16, NY), 1) < NY - 1).astype(F32)
    row_keep = (row_block < 15).astype(F32)
    depth_keep = jnp.logical_or(c == 0, z < 3).astype(F32)

    def edges(slot):
        col = slot * SLAB
        next_col = col + SLAB if slot % 2 == 0 else ZCOL + (slot // 2) * OWN

        def group(g, acc):
            rows = pl.ds(pl.multiple_of(g * 16, 16), 16)

            def load(ref, start):
                return ref[rows, pl.ds(start, NY)].astype(F32)

            def diffs(ref, r, here):
                ahead = load(ref, col + (r + 1) * NY)
                side = pltpu.roll(here, NY - 1, 1)
                below = load(ref, next_col + r * NY)
                return ahead, ahead - here, side - here, below - here

            new = list(acc)
            u = load(field, col)
            v = [load(psi.at[k], col) for k in range(2)]
            for r in range(ROWS):
                u_next, ux, uy, uz = diffs(field, r, u)
                uy = uy * lane_keep
                if r == ROWS - 1:
                    ux = ux * row_keep
                if slot == 3:
                    uz = uz * depth_keep
                for k in range(2):
                    v_next, vx, vy, vz = diffs(psi.at[k], r, v[k])
                    term = ux * vx + uy * vy + uz * vz
                    new[k * ROWS + r] = new[k * ROWS + r] + term[:8] + term[8:]
                    v[k] = v_next
                u = u_next
            return tuple(new)

        acc = lax.fori_loop(0, ELECTRODES // 16, group, tuple(jnp.zeros((8, NY), F32) for _ in range(2 * ROWS)))
        for k in range(2):
            for r in range(ROWS):
                sens[slot // 2, k, slot % 2, r:r + 1, :] = jnp.sum(acc[k * ROWS + r], axis=0, keepdims=True)

    for slot in range(4):
        edges(slot)

    swap = pltpu.make_async_remote_copy(
        src_ref=sens.at[1 - xl], dst_ref=other, send_sem=ps_sem.at[0], recv_sem=pr_sem.at[0],
        device_id=device_of(xh * 2 + 1 - xl, y, z, c), device_id_type=MESH)
    swap.start()
    mine[...] = sens[xl]
    swap.wait()
    first = jnp.where(xl == 0, mine[...], other[...])
    second = jnp.where(xl == 0, other[...], mine[...])
    full = jnp.concatenate([first, second], axis=2)
    gradient = -(cond[...] * inside[...].astype(F32))[None] * full
    grad_out[...] = gradient
    depth0 = (s * 2).astype(F32)
    weight0 = 1.0 + 2.0 * depth0 / 32.0
    weight1 = 1.0 + 2.0 * (depth0 + 1.0) / 32.0
    run0 = weight0 * gradient[:, 0] * gradient[:, 0]
    run1 = run0 + weight1 * gradient[:, 1] * gradient[:, 1]
    totals[16] = run1

    def total_copy(i):
        return pltpu.make_async_remote_copy(
            src_ref=totals.at[16], dst_ref=totals.at[s], send_sem=ts_sem.at[i], recv_sem=tr_sem.at[s],
            device_id=(e, i), device_id_type=MESH)

    def total_arrival(i):
        return pltpu.make_async_remote_copy(
            src_ref=totals.at[16], dst_ref=totals.at[i], send_sem=ts_sem.at[i], recv_sem=tr_sem.at[i],
            device_id=(e, i), device_id_type=MESH)

    lax.fori_loop(s + 1, 16, lambda i, _: (total_copy(i).start(), 0)[1], 0)

    def add_total(i, before):
        total_arrival(i).wait_recv()
        return before + totals[i]
    prefix = lax.fori_loop(0, s, add_total, jnp.zeros((2, 8, NY), F32))
    scaled_out[:, 0] = gradient[:, 0] / jnp.sqrt(1.0 + (prefix + run0) / (depth0 + 1.0))
    scaled_out[:, 1] = gradient[:, 1] / jnp.sqrt(1.0 + (prefix + run1) / (depth0 + 2.0))

    lax.fori_loop(s + 1, 16, lambda i, _: (total_copy(i).wait_send(), 0)[1], 0)
    for p in range(2):
        for i in range(n_off):
            slab_copy(p, i).wait_send()
    for j in range(2):
        halo_copy(j).wait_send()
    for d in (1, 3, 2):
        w_copy(d).wait_send()
    for d in range(4):
        w_across(d).wait_send()


def per_device(potentials, measurements, residuals, conductivity, inside):
    vmem = pl.BlockSpec(memory_space=pltpu.VMEM)
    dma = pltpu.SemaphoreType.DMA
    shape = jax.ShapeDtypeStruct((2, 2, 8, NY), F32)
    n_off = len(OFFSETS)
    gradient, scaled = pl.pallas_call(
        kernel_body,
        out_shape=(shape, shape),
        in_specs=[pl.BlockSpec(memory_space=pl.ANY), vmem, vmem, vmem, vmem],
        out_specs=(vmem, vmem),
        scratch_shapes=[
            pltpu.VMEM((2, 128, 8192), F32),
            pltpu.VMEM((2, 128, 8192 + NY), BF),
            pltpu.VMEM((ELECTRODES, 4 * SLAB + 2 * OWN), BF),
            pltpu.VMEM((2, ELECTRODES, ELECTRODES), BF),
            pltpu.VMEM((2, 256, 512), F32),
            pltpu.VMEM((2, ELECTRODES, 4 * SLAB + 2 * OWN), BF),
            pltpu.VMEM((2, 2, 2, ROWS, NY), F32),
            pltpu.VMEM((2, 2, ROWS, NY), F32),
            pltpu.VMEM((2, 2, ROWS, NY), F32),
            pltpu.VMEM((17, 2, 8, NY), F32),
            dma((2, 4)), dma((2,)), dma((2, n_off)), dma((2, n_off)), dma((2,)), dma((2,)),
            dma((4,)), dma((4,)), dma((4,)), dma((4,)), dma((1,)), dma((1,)), dma((16,)), dma((16,)),
        ],
        compiler_params=pltpu.CompilerParams(collective_id=0, has_side_effects=True, vmem_limit_bytes=60 << 20),
        name="misfit_gradient",
    )(potentials, measurements.T, residuals, conductivity.reshape(2, 8, NY), inside.reshape(2, 8, NY))
    return gradient.reshape(2, 2, 1024), scaled.reshape(2, 2, 1024)


def solution(mesh):
    return jax.shard_map(
        per_device,
        mesh=mesh,
        in_specs=(P("space", "elec", None), P(), P(), P("space", "elec"), P("space", "elec")),
        out_specs=(P(None, "space", "elec"), P(None, "space", "elec")),
        check_vma=False,
    )
```

```python
import functools

import jax
import jax.numpy as jnp
from jax import lax
from jax.experimental import pallas as pl
from jax.experimental.pallas import tpu as pltpu
from jax.sharding import PartitionSpec as P

ELECTRODES = 1024
NY = 128
ROWS = 4
SLAB = (ROWS + 1) * NY
OWN = ROWS * NY
MESH = pl.DeviceIdType.MESH
BF = jnp.bfloat16
F32 = jnp.float32
OFFSETS = [(2, 2), (1, 0), (0, 3), (2, 1), (3, 0), (0, 1), (1, 2), (3, 3), (2, 0), (0, 2), (1, 1), (3, 2), (2, 3), (1, 3), (3, 1)]
QUAD_CHUNK = 1024
GROUP = 256
ADJ_ROWS = 1024
ZCOL = 4 * SLAB


def device_of(x, y, z, c):
    return (lax.div(x, 2) * 4 + y, z * 4 + lax.rem(x, 2) * 2 + c)


def kernel_body(pot, quads, resid, cond, inside, grad_out, scaled_out,
                stage, send, field, weights, sym, wacc, adj, cond_t, q_own, q_ahead, cross, q_row, q_row_in, q_depth_in,
                sens, other, totals,
                stage_sem, own_sem, out_sem, in_sem, zs_sem, zr_sem, ws_sem, wr_sem, ds_sem, dr_sem,
                ps_sem, pr_sem, ts_sem, tr_sem, qs_sem, qr_sem):
    e = lax.axis_index("elec")
    s = lax.axis_index("space")
    y = lax.rem(e, 4)
    xh = lax.div(e, 4)
    c = lax.rem(s, 2)
    xl = lax.rem(lax.div(s, 2), 2)
    z = lax.div(s, 4)
    x = xh * 2 + xl
    n_off = len(OFFSETS)

    cells = pot.shape[2]
    quarter = cells // 4

    def stage_copy(p, q):
        cols = pl.ds(q * quarter, quarter)
        return pltpu.make_async_copy(pot.at[p, :, cols], stage.at[p, :, cols], stage_sem.at[p, q])

    for p in range(2):
        for q in range(4):
            stage_copy(p, q).start()

    bar = pltpu.get_barrier_semaphore()
    for dx, dy in OFFSETS:
        pl.semaphore_signal(bar, inc=1, device_id=device_of(lax.rem(x + dx, 4), lax.rem(y + dy, 4), z, c), device_id_type=MESH)
    for i in range(1, 16):
        pl.semaphore_signal(bar, inc=1, device_id=(e, lax.rem(s + i, 16)), device_id_type=MESH)

    pieces = [(0, 0, 5), (1, 0, 3), (1, 3, 2)]

    def slab_copy(m, i):
        p, row0, rows = pieces[m]
        dx, dy = OFFSETS[i]
        tx = lax.rem(x + dx, 4)
        ty = lax.rem(y + dy, 4)
        block = (lax.div(tx, 2) * 4 + ty) * 2 + lax.rem(tx, 2)
        return pltpu.make_async_remote_copy(
            src_ref=send.at[p, :, pl.ds(pl.multiple_of(block * OWN + row0 * NY, 128), rows * NY)],
            dst_ref=field.at[pl.ds(pl.multiple_of(e * 128, 128), 128), pl.ds(pl.multiple_of((xl * 2 + p) * SLAB + row0 * NY, 128), rows * NY)],
            send_sem=out_sem.at[m, i], recv_sem=in_sem.at[m, i],
            device_id=device_of(tx, ty, z, c), device_id_type=MESH)

    row_block = e * 2 + xl

    def own_copy(p):
        return pltpu.make_async_copy(
            send.at[p, :, pl.ds(pl.multiple_of(row_block * OWN, OWN), SLAB)],
            field.at[pl.ds(pl.multiple_of(e * 128, 128), 128), pl.ds(pl.multiple_of((xl * 2 + p) * SLAB, 128), SLAB)],
            own_sem.at[p])

    for p in range(2):
        send[p, :, pl.ds(cells, NY)] = jnp.zeros((128, NY), BF)
        for q in range(4):
            stage_copy(p, q).wait()

            def cast(i, _):
                rows = pl.ds(pl.multiple_of(i * 16, 16), 16)
                cols = pl.ds(q * quarter, quarter)
                send[p, rows, cols] = stage[p, rows, cols].astype(BF)
                return 0
            lax.fori_loop(0, 8, cast, 0)
        if p == 0:
            pl.semaphore_wait(bar, n_off + 15)
        for m in ((0,), (1, 2))[p]:
            for i in range(n_off):
                slab_copy(m, i).start()
        own_copy(p).start()

    quarter_f = 256
    half_e = 512
    wacc[...] = jnp.zeros_like(wacc)
    f_ids = z * quarter_f + lax.broadcasted_iota(jnp.int32, (quarter_f, QUAD_CHUNK), 0)
    e_ids = c * half_e + lax.broadcasted_iota(jnp.int32, (half_e, QUAD_CHUNK), 0)

    def add_quads(i, _):
        cols = pl.ds(pl.multiple_of(i * QUAD_CHUNK, QUAD_CHUNK), QUAD_CHUNK)
        left = (jnp.where(quads[2:3, cols] == f_ids, 1.0, 0.0) - jnp.where(quads[3:4, cols] == f_ids, 1.0, 0.0)).astype(BF)
        right = (jnp.where(quads[0:1, cols] == e_ids, 1.0, 0.0) - jnp.where(quads[1:2, cols] == e_ids, 1.0, 0.0)).astype(BF)
        for k in range(2):
            r = resid[k:k + 1, cols]
            hi = r.astype(BF)
            lo = (r - hi.astype(F32)).astype(BF)
            for part in (hi, lo):
                wacc[k] += lax.dot_general(left * part, right, (((1,), (1,)), ((), ())), preferred_element_type=F32)
        return 0
    lax.fori_loop(0, quads.shape[1] // QUAD_CHUNK, add_quads, 0)

    def block_of(zz, cc):
        return weights.at[:, pl.ds(pl.multiple_of(zz * quarter_f, quarter_f), quarter_f), pl.ds(pl.multiple_of(cc * half_e, half_e), half_e)]

    weights[:, pl.ds(pl.multiple_of(z * quarter_f, quarter_f), quarter_f), pl.ds(pl.multiple_of(c * half_e, half_e), half_e)] = wacc[...].astype(BF)

    def w_copy(d):
        tz = lax.rem(z + d, 4)
        return pltpu.make_async_remote_copy(
            src_ref=block_of(z, c), dst_ref=block_of(z, c), send_sem=ws_sem.at[d], recv_sem=wr_sem.at[d],
            device_id=device_of(x, y, tz, c), device_id_type=MESH)

    def w_across(d):
        zz = lax.rem(z + 4 - d, 4)
        return pltpu.make_async_remote_copy(
            src_ref=block_of(zz, c), dst_ref=block_of(zz, c), send_sem=ds_sem.at[d], recv_sem=dr_sem.at[d],
            device_id=device_of(x, y, z, 1 - c), device_id_type=MESH)

    for d in (1, 3, 2):
        w_copy(d).start()
    w_across(0).start()

    for i in range(n_off):
        slab_copy(0, i).wait_recv()
    own_copy(0).wait()

    def halo_copy(j):
        slot = jnp.where(c == 0, 2 - 2 * j, 2 * j)
        if j == 0:
            target = device_of(x, y, z, 1 - c)
        else:
            target = device_of(x, y, jnp.where(c == 0, lax.rem(z + 3, 4), z), 1 - c)
        return pltpu.make_async_remote_copy(
            src_ref=field.at[:, pl.ds(pl.multiple_of(slot * SLAB, 128), OWN)],
            dst_ref=field.at[:, pl.ds(ZCOL + j * OWN, OWN)],
            send_sem=zs_sem.at[j], recv_sem=zr_sem.at[j], device_id=target, device_id_type=MESH)

    for j in (1, 0):
        halo_copy(j).start()

    for d in (1, 3, 2):
        w_copy(d).wait_recv()
        w_across(d).start()
    for d in (0, 1, 3, 2):
        w_across(d).wait_recv()

    def symmetrize(i, _):
        k = lax.div(i, 16)
        rows = pl.ds(pl.multiple_of(lax.rem(lax.div(i, 4), 4) * 256, 256), 256)
        cols = pl.ds(pl.multiple_of(lax.rem(i, 4) * 256, 256), 256)
        sym[k, rows, cols] = (weights[k, rows, cols].astype(F32) + weights[k, cols, rows].astype(F32).T).astype(BF)
        return 0
    lax.fori_loop(0, 32, symmetrize, 0)

    lane_keep = (lax.broadcasted_iota(jnp.int32, (8, NY), 1) < NY - 1).astype(F32)
    row_keep = (row_block < 15).astype(F32)
    depth_keep = jnp.logical_or(c == 0, z < 3).astype(F32)

    def work(slot, r0):
        col = slot * SLAB
        odd = slot % 2 == 1
        cols = pl.ds(col + r0 * NY, 2 * NY)

        def block(i, _):
            k = lax.div(i, 1024 // ADJ_ROWS)
            rows = pl.ds(pl.multiple_of(lax.rem(i, 1024 // ADJ_ROWS) * ADJ_ROWS, ADJ_ROWS), ADJ_ROWS)
            adj[k, rows, :] = jnp.dot(sym[k, rows, :], field[:, cols], preferred_element_type=F32)
            return 0
        lax.fori_loop(0, 2048 // ADJ_ROWS, block, 0)

        def group(g, acc):
            rows = pl.ds(pl.multiple_of(g * GROUP, GROUP), GROUP)

            def load(start):
                return field[rows, pl.ds(start, NY)].astype(F32)

            new = list(acc)
            n = 0
            u = load(col + r0 * NY)
            for r in (r0, r0 + 1):
                ahead = load(col + (r + 1) * NY)
                near = (ahead * row_keep if r == ROWS - 1 else ahead) + pltpu.roll(u, NY - 1, 1) * lane_keep[:1]
                if odd:
                    below = load(ZCOL + (slot // 2) * OWN + r * NY)
                    near = near + (below * depth_keep if slot == 3 else below)
                    above = load(col - SLAB + r * NY)
                for k in range(2):
                    v = adj[k, rows, pl.ds((r - r0) * NY, NY)]
                    for other_u in ((u, near, above) if odd else (u, near)):
                        t = other_u * v
                        new[n] = new[n] + jnp.sum(t.reshape(GROUP // 8, 8, NY), axis=0)
                        n += 1
                u = ahead
            return tuple(new)

        per = 3 if odd else 2
        acc = lax.fori_loop(0, ELECTRODES // GROUP, group, tuple(jnp.zeros((8, NY), F32) for _ in range(4 * per)))
        n = 0
        for r in (r0, r0 + 1):
            for k in range(2):
                row = k * ROWS + r
                total = [jnp.sum(acc[n + t], axis=0, keepdims=True) for t in range(per)]
                n += per
                q = 0.5 * total[0]
                q_own[slot, row:row + 1, :] = q
                if r > 0:
                    q_ahead[slot, row - 1:row, :] = q
                else:
                    q_row[slot * 2 + k:slot * 2 + k + 1, :] = q
                cross[slot, row:row + 1, :] = total[1]
                if odd:
                    cross[slot - 1, row:row + 1, :] += total[2]

    def q_depth_copy(j):
        slot = jnp.where(c == 0, 2 - 2 * j, 2 * j)
        if j == 0:
            target = device_of(x, y, z, 1 - c)
        else:
            target = device_of(x, y, jnp.where(c == 0, lax.rem(z + 3, 4), z), 1 - c)
        return pltpu.make_async_remote_copy(
            src_ref=q_own.at[slot], dst_ref=q_depth_in.at[j], send_sem=qs_sem.at[j], recv_sem=qr_sem.at[j],
            device_id=target, device_id_type=MESH)

    def q_row_copy():
        before = lax.rem(row_block + 15, 16)
        be = lax.div(before, 2)
        return pltpu.make_async_remote_copy(
            src_ref=q_row, dst_ref=q_row_in, send_sem=qs_sem.at[2], recv_sem=qr_sem.at[2],
            device_id=(be, z * 4 + lax.rem(before, 2) * 2 + c), device_id_type=MESH)

    for slot in (0, 2):
        for r0 in (0, 2):
            work(slot, r0)
    for j in (0, 1):
        q_depth_copy(j).start()
    for j in range(2):
        halo_copy(j).wait_recv()
    for i in range(n_off):
        slab_copy(1, i).wait_recv()
    own_copy(1).wait()
    for slot in (1, 3):
        work(slot, 0)
    q_row_copy().start()
    for i in range(n_off):
        slab_copy(2, i).wait_recv()
    for slot in (1, 3):
        work(slot, 2)
    for j in range(2):
        q_depth_copy(j).wait_recv()
    q_row_copy().wait_recv()

    edge_lane = lane_keep
    sub_row = lax.rem(lax.broadcasted_iota(jnp.int32, (8, NY), 0), ROWS)
    x_valid = jnp.where(sub_row == ROWS - 1, row_keep, 1.0)
    for slot in range(4):
        for k in range(2):
            row = k * ROWS + ROWS - 1
            q_ahead[slot, row:row + 1, :] = q_row_in[slot * 2 + k:slot * 2 + k + 1, :] * row_keep
        z_valid = depth_keep if slot == 3 else 1.0
        q = q_own[slot]
        q_below = q_own[slot + 1] if slot % 2 == 0 else q_depth_in[slot // 2] * z_valid
        sens[slot] = (x_valid + edge_lane + z_valid) * q + q_ahead[slot] + pltpu.roll(q, NY - 1, 1) * edge_lane + q_below - cross[slot]

    swap = pltpu.make_async_remote_copy(
        src_ref=sens.at[pl.ds(2 * (1 - xl), 2)], dst_ref=other, send_sem=ps_sem.at[0], recv_sem=pr_sem.at[0],
        device_id=device_of(xh * 2 + 1 - xl, y, z, c), device_id_type=MESH)
    swap.start()
    rate = -(cond[...] * inside[...].astype(F32))
    for p in range(2):
        for r in range(8):
            cond_t[p, r:r + 1, :] = rate[p:p + 1, r * NY:(r + 1) * NY]
    mine = sens[pl.ds(2 * xl, 2)]
    swap.wait()
    theirs = other[...]
    first = jnp.where(xl == 0, mine, theirs)
    second = jnp.where(xl == 0, theirs, mine)
    gradient = [[cond_t[p] * jnp.concatenate([first[p, k * ROWS:(k + 1) * ROWS], second[p, k * ROWS:(k + 1) * ROWS]], axis=0)
                 for p in range(2)] for k in range(2)]
    depth0 = (s * 2).astype(F32)
    weight0 = 1.0 + 2.0 * depth0 / 32.0
    weight1 = 1.0 + 2.0 * (depth0 + 1.0) / 32.0
    run0 = [weight0 * gradient[k][0] * gradient[k][0] for k in range(2)]
    run1 = [run0[k] + weight1 * gradient[k][1] * gradient[k][1] for k in range(2)]
    for k in range(2):
        totals[16, k] = run1[k]

    def total_copy(i):
        return pltpu.make_async_remote_copy(
            src_ref=totals.at[16], dst_ref=totals.at[s], send_sem=ts_sem.at[i], recv_sem=tr_sem.at[s],
            device_id=(e, i), device_id_type=MESH)

    def total_arrival(i):
        return pltpu.make_async_remote_copy(
            src_ref=totals.at[16], dst_ref=totals.at[i], send_sem=ts_sem.at[i], recv_sem=tr_sem.at[i],
            device_id=(e, i), device_id_type=MESH)

    lax.fori_loop(s + 1, 16, lambda i, _: (total_copy(i).start(), 0)[1], 0)

    def add_total(i, before):
        total_arrival(i).wait_recv()
        return before + totals[i]
    prefix = lax.fori_loop(0, s, add_total, jnp.zeros((2, 8, NY), F32))
    for k in range(2):
        for p, run in ((0, run0[k]), (1, run1[k])):
            g = gradient[k][p]
            scaled = g / jnp.sqrt(1.0 + (prefix[k] + run) / (depth0 + (p + 1.0)))
            for r in range(8):
                grad_out[k, p:p + 1, r * NY:(r + 1) * NY] = g[r:r + 1]
                scaled_out[k, p:p + 1, r * NY:(r + 1) * NY] = scaled[r:r + 1]

    lax.fori_loop(s + 1, 16, lambda i, _: (total_copy(i).wait_send(), 0)[1], 0)
    for m in range(3):
        for i in range(n_off):
            slab_copy(m, i).wait_send()
    for j in range(2):
        q_depth_copy(j).wait_send()
    q_row_copy().wait_send()
    for j in range(2):
        halo_copy(j).wait_send()
    for d in (1, 3, 2):
        w_copy(d).wait_send()
    for d in range(4):
        w_across(d).wait_send()


def per_device(potentials, measurements, residuals, conductivity, inside):
    vmem = pl.BlockSpec(memory_space=pltpu.VMEM)
    dma = pltpu.SemaphoreType.DMA
    shape = jax.ShapeDtypeStruct((2, 2, 1024), F32)
    n_off = len(OFFSETS)
    tile = (8, NY)
    return pl.pallas_call(
        kernel_body,
        out_shape=(shape, shape),
        in_specs=[pl.BlockSpec(memory_space=pl.ANY), vmem, vmem, vmem, vmem],
        out_specs=(vmem, vmem),
        scratch_shapes=[
            pltpu.VMEM((2, 128, 8192), F32),
            pltpu.VMEM((2, 128, 8192 + NY), BF),
            pltpu.VMEM((ELECTRODES, 4 * SLAB + 2 * OWN), BF),
            pltpu.VMEM((2, ELECTRODES, ELECTRODES), BF),
            pltpu.VMEM((2, ELECTRODES, ELECTRODES), BF),
            pltpu.VMEM((2, 256, 512), F32),
            pltpu.VMEM((2, ELECTRODES, 2 * NY), F32),
            pltpu.VMEM((2,) + tile, F32),
            pltpu.VMEM((4,) + tile, F32),
            pltpu.VMEM((4,) + tile, F32),
            pltpu.VMEM((4,) + tile, F32),
            pltpu.VMEM(tile, F32),
            pltpu.VMEM(tile, F32),
            pltpu.VMEM((2,) + tile, F32),
            pltpu.VMEM((4,) + tile, F32),
            pltpu.VMEM((2,) + tile, F32),
            pltpu.VMEM((17, 2) + tile, F32),
            dma((2, 4)), dma((2,)), dma((3, n_off)), dma((3, n_off)), dma((2,)), dma((2,)),
            dma((4,)), dma((4,)), dma((4,)), dma((4,)), dma((1,)), dma((1,)), dma((16,)), dma((16,)), dma((3,)), dma((3,)),
        ],
        compiler_params=pltpu.CompilerParams(collective_id=0, has_side_effects=True, vmem_limit_bytes=60 << 20),
        name="misfit_gradient",
    )(potentials, measurements.T, residuals, conductivity, inside)


def solution(mesh):
    return jax.shard_map(
        per_device,
        mesh=mesh,
        in_specs=(P("space", "elec", None), P(), P(), P("space", "elec"), P("space", "elec")),
        out_specs=(P(None, "space", "elec"), P(None, "space", "elec")),
        check_vma=False,
    )
```

```python
import functools

import jax
import jax.numpy as jnp
from jax import lax
from jax.experimental import pallas as pl
from jax.experimental.pallas import tpu as pltpu
from jax.sharding import PartitionSpec as P

ELECTRODES = 1024
NY = 128
ROWS = 4
SLAB = (ROWS + 1) * NY
OWN = ROWS * NY
MESH = pl.DeviceIdType.MESH
BF = jnp.bfloat16
F32 = jnp.float32
QUAD_CHUNK = 2048
XROWS = 4 * ROWS + 1
GROUP = 256
ADJ_ROWS = 1024
ZCOL = 4 * SLAB


def device_of(x, y, z, c):
    return (lax.div(x, 2) * 4 + y, z * 4 + lax.rem(x, 2) * 2 + c)


def kernel_body(pot, quads, resid, cond, inside, grad_out, scaled_out,
                stage, send, mid, field, weights, sym, wacc, adj, cond_t, q_own, q_ahead, cross, q_row, q_row_in, q_depth_in,
                sens, other, totals,
                stage_sem, loc_sem, xs_sem, xr_sem, ys_sem, yr_sem, zs_sem, zr_sem, ws_sem, wr_sem, ds_sem, dr_sem,
                ps_sem, pr_sem, ts_sem, tr_sem, qs_sem, qr_sem):
    e = lax.axis_index("elec")
    s = lax.axis_index("space")
    y = lax.rem(e, 4)
    xh = lax.div(e, 4)
    c = lax.rem(s, 2)
    xl = lax.rem(lax.div(s, 2), 2)
    z = lax.div(s, 4)
    x = xh * 2 + xl
    row_block = x * 4 + y

    cells = pot.shape[2]
    quarter = cells // 4

    def stage_copy(p, q):
        cols = pl.ds(q * quarter, quarter)
        return pltpu.make_async_copy(pot.at[p, :, cols], stage.at[p, :, cols], stage_sem.at[p, q])

    for p in range(2):
        for q in range(4):
            stage_copy(p, q).start()

    def owner(j):
        return device_of(lax.div(x, 2) * 2 + j, 2 * lax.rem(x, 2) + lax.div(y, 2), z, c)

    def owner_is_me(j):
        return jnp.logical_and(xl == j, y == 2 * xl + lax.div(y, 2))

    def holder(h):
        return device_of(2 * xh + lax.div(y, 2), 2 * lax.rem(y, 2) + h, z, c)

    def holder_is_me(h):
        return jnp.logical_and(x == 2 * xh + lax.div(y, 2), y == 2 * lax.rem(y, 2) + h)

    def row_device(b):
        return device_of(lax.div(b, 4), lax.rem(b, 4), z, c)

    bar = pltpu.get_barrier_semaphore()

    def greet(device):
        pl.semaphore_signal(bar, inc=1, device_id=device, device_id_type=MESH)

    for d in range(1, 4):
        greet(device_of(lax.rem(x + d, 4), y, z, c))
        greet(device_of(x, lax.rem(y + d, 4), z, c))
    greet(row_device(lax.rem(row_block + 1, 16)))
    for i in range(1, 16):
        greet((e, lax.rem(s + i, 16)))
    targets = 0
    for j in range(2):
        @pl.when(jnp.logical_not(holder_is_me(j)))
        def _():
            greet(holder(j))
        targets = targets + jnp.where(owner_is_me(j), 0, 1)

    def x_parts():
        return ((0, 64), (64, 64))

    def x_copy(p, d, h):
        tx = lax.rem(x + 4 - d, 4)
        rows = pl.ds(*x_parts()[h])
        return pltpu.make_async_remote_copy(
            src_ref=send.at[p, rows, pl.ds(pl.multiple_of(tx * (4 * OWN), 128), XROWS * NY)], dst_ref=mid.at[p, d - 1, rows],
            send_sem=xs_sem.at[p, d, h], recv_sem=xr_sem.at[p, d, h],
            device_id=device_of(tx, y, z, c), device_id_type=MESH)

    def pieces(p, d):
        if d == 0:
            return ((0, 0, 5),)
        if p == 1 and d == 2:
            return ((0, 0, 5), (1, 0, 3), (1, 3, 2))
        return ((0, 0, 5), (1, 0, 5))

    def slab(p, d, ty, first_e, count, row0, rows):
        xs = lax.rem(x + d, 4)
        es = pl.ds(first_e, count)
        if d == 0:
            src = send.at[p, es, pl.ds(pl.multiple_of((x * 4 + ty) * OWN + row0 * NY, 128), rows * NY)]
        else:
            src = mid.at[p, d - 1, es, pl.ds(pl.multiple_of(ty * OWN + row0 * NY, 128), rows * NY)]
        dst = field.at[pl.ds(pl.multiple_of(lax.div(xs, 2) * 512 + y * 128 + first_e, 64), count),
                       pl.ds(pl.multiple_of((lax.rem(xs, 2) * 2 + p) * SLAB + row0 * NY, 128), rows * NY)]
        return src, dst

    def y_copy(p, d, m, dy):
        ty = lax.rem(y + dy, 4)
        h, row0, rows = pieces(p, d)[m]
        src, dst = slab(p, d, ty, *(x_parts()[h] if d > 0 else (0, 128)), row0, rows)
        return pltpu.make_async_remote_copy(
            src_ref=src, dst_ref=dst, send_sem=ys_sem.at[p, d, m, dy], recv_sem=yr_sem.at[p, d, m, dy],
            device_id=device_of(x, ty, z, c), device_id_type=MESH)

    def local_copy(p, d):
        return pltpu.make_async_copy(*slab(p, d, y, 0, 128, 0, 5), loc_sem.at[p, d])

    def y_start(p, d, h=0):
        for m, piece in enumerate(pieces(p, d)):
            if piece[0] == h:
                for dy in (1, 3, 2):
                    y_copy(p, d, m, dy).start()
        if d == 0 or h == len(x_parts()) - 1:
            local_copy(p, d).start()

    def y_wait(p, d, chosen=None):
        for m in range(len(pieces(p, d))) if chosen is None else chosen:
            for dy in (1, 3, 2):
                y_copy(p, d, m, dy).wait_recv()
        if chosen is None or 0 in chosen:
            local_copy(p, d).wait()

    def pass_on(p, d, h=0):
        x_copy(p, d, h).wait_recv()
        y_start(p, d, h)

    for p in range(2):
        send[p, :, pl.ds(cells, NY)] = jnp.zeros((128, NY), BF)
        for q in range(4):
            stage_copy(p, q).wait()

            def cast(i, _):
                rows = pl.ds(pl.multiple_of(i * 16, 16), 16)
                cols = pl.ds(q * quarter, quarter)
                send[p, rows, cols] = stage[p, rows, cols].astype(BF)
                return 0
            lax.fori_loop(0, 8, cast, 0)
        if p == 0:
            pl.semaphore_wait(bar, 22 + targets)
        for d in (1, 3, 2):
            for h in range(len(x_parts())):
                x_copy(p, d, h).start()
        y_start(p, 0)

    quarter_f = 256
    half_e = 512
    def one_hot(plus, minus, base, count):
        parts = []
        for b in range(0, count, 256):
            ids = lax.broadcasted_iota(jnp.int32, (256, QUAD_CHUNK), 0).astype(F32).astype(BF)
            hit = (plus - (base + b)).astype(F32).astype(BF) == ids
            miss = (minus - (base + b)).astype(F32).astype(BF) == ids
            one = jnp.ones((), BF)
            parts.append(jnp.where(hit, one, jnp.where(miss, -one, jnp.zeros((), BF))))
        return parts[0] if len(parts) == 1 else jnp.concatenate(parts, axis=0)

    def add_quads(part, first, last):
        def step(i, _):
            cols = pl.ds(pl.multiple_of(i * QUAD_CHUNK, QUAD_CHUNK), QUAD_CHUNK)
            left = one_hot(quads[2:3, cols], quads[3:4, cols], z * quarter_f, quarter_f)
            right = one_hot(quads[0:1, cols], quads[1:2, cols], c * half_e + part * 256, 256)
            parts = []
            for k in range(2):
                r = resid[k:k + 1, cols]
                hi = r.astype(BF)
                parts += [left * hi, left * (r - hi.astype(F32)).astype(BF)]
            both = lax.dot_general(jnp.concatenate(parts, axis=0), right, (((1,), (1,)), ((), ())), preferred_element_type=F32)
            for k in range(2):
                wacc[part, k] += both[k * 512:k * 512 + 256] + both[k * 512 + 256:k * 512 + 512]
            return 0
        if first == 0:
            wacc[part] = jnp.zeros(wacc.shape[1:], F32)
        lax.fori_loop(first, last, step, 0)

    def block_of(part, zz, cc):
        return weights.at[:, pl.ds(pl.multiple_of(zz * quarter_f, quarter_f), quarter_f),
                          pl.ds(pl.multiple_of(cc * half_e + part * 256, 256), 256)]

    def w_copy(part, d):
        zz = lax.rem(z + 3, 4) if d == 2 else z
        step = 3 if d == 3 else 1
        return pltpu.make_async_remote_copy(
            src_ref=block_of(part, zz, c), dst_ref=block_of(part, zz, c), send_sem=ws_sem.at[part, d], recv_sem=wr_sem.at[part, d],
            device_id=device_of(x, y, lax.rem(z + step, 4), c), device_id_type=MESH)

    def w_across(part, d):
        zz = lax.rem(z + 4 - d, 4)
        return pltpu.make_async_remote_copy(
            src_ref=block_of(part, zz, c), dst_ref=block_of(part, zz, c), send_sem=ds_sem.at[part, d], recv_sem=dr_sem.at[part, d],
            device_id=device_of(x, y, z, 1 - c), device_id_type=MESH)

    def w_share(part):
        weights[:, pl.ds(pl.multiple_of(z * quarter_f, quarter_f), quarter_f),
                pl.ds(pl.multiple_of(c * half_e + part * 256, 256), 256)] = wacc[part].astype(BF)
        w_copy(part, 1).start()
        w_copy(part, 3).start()
        w_across(part, 0).start()

    def w_forward(part):
        w_copy(part, 1).wait_recv()
        w_copy(part, 2).start()
        w_across(part, 1).start()
        w_copy(part, 3).wait_recv()
        w_across(part, 3).start()

    def w_last(part):
        w_copy(part, 2).wait_recv()
        w_across(part, 2).start()

    chunks = quads.shape[1] // QUAD_CHUNK
    def halo_target(pair):
        down = jnp.logical_and(c == 0, pair == 0)
        j = jnp.where(c == 0, 1 - pair, pair)
        return j, device_of(x, y, jnp.where(down, lax.rem(z + 3, 4), z), 1 - c)

    def halo_copy(d):
        xs = lax.rem(x + d, 4)
        pair = lax.rem(xs, 2)
        half = lax.div(xs, 2)
        j, target = halo_target(pair)
        rows = pl.ds(pl.multiple_of(half * 512, 512), 512)
        return pltpu.make_async_remote_copy(
            src_ref=field.at[rows, pl.ds(pl.multiple_of(pair * (2 * SLAB), 128), OWN)],
            dst_ref=field.at[rows, pl.ds(pl.multiple_of(ZCOL + j * OWN, 128), OWN)],
            send_sem=zs_sem.at[d], recv_sem=zr_sem.at[j * 2 + half], device_id=target, device_id_type=MESH)

    def halo_arrival(j, half):
        return pltpu.make_async_remote_copy(
            src_ref=field.at[pl.ds(0, 512), pl.ds(0, OWN)], dst_ref=field.at[pl.ds(half * 512, 512), pl.ds(ZCOL + j * OWN, OWN)],
            send_sem=zs_sem.at[0], recv_sem=zr_sem.at[j * 2 + half], device_id=device_of(x, y, z, 1 - c), device_id_type=MESH)

    def first_planes(d):
        y_wait(0, d)
        halo_copy(d).start()

    def near_on(p, h):
        pass_on(p, 1, h)
        pass_on(p, 3, h)

    eighth = chunks // 8
    add_quads(0, 0, 5 * eighth)
    near_on(0, 0)
    add_quads(0, 5 * eighth, chunks)
    w_share(0)
    add_quads(1, 0, 2 * eighth)
    near_on(0, 1)
    add_quads(1, 2 * eighth, 5 * eighth)
    w_forward(0)
    add_quads(1, 5 * eighth, 7 * eighth)
    pass_on(0, 2, 0)
    add_quads(1, 7 * eighth, chunks)
    w_share(1)
    w_last(0)
    pass_on(0, 2, 1)
    w_forward(1)
    first_planes(0)
    first_planes(1)
    first_planes(3)
    near_on(1, 0)
    w_last(1)
    for part in range(2):
        for d in range(4):
            w_across(part, d).wait_recv()

    def symmetrize(i, _):
        k = lax.div(i, 16)
        rows = pl.ds(pl.multiple_of(lax.rem(lax.div(i, 4), 4) * 256, 256), 256)
        cols = pl.ds(pl.multiple_of(lax.rem(i, 4) * 256, 256), 256)
        sym[k, rows, cols] = (weights[k, rows, cols].astype(F32) + weights[k, cols, rows].T.astype(F32)).astype(BF)
        return 0
    lax.fori_loop(0, 16, symmetrize, 0, unroll=4)
    near_on(1, 1)
    lax.fori_loop(16, 32, symmetrize, 0, unroll=4)
    first_planes(2)

    lane_keep = (lax.broadcasted_iota(jnp.int32, (8, NY), 1) < NY - 1).astype(F32)
    row_keep = (row_block < 15).astype(F32)
    depth_keep = jnp.logical_or(c == 0, z < 3).astype(F32)

    def work(pair, p, r0):
        slot = pair * 2 + p
        col = slot * SLAB
        odd = p == 1
        cols = pl.ds(pl.multiple_of(col + r0 * NY, 128), 2 * NY)
        z_keep = jnp.where(pair == 1, depth_keep, 1.0)

        def block(i, _):
            k = lax.div(i, 1024 // ADJ_ROWS)
            rows = pl.ds(pl.multiple_of(lax.rem(i, 1024 // ADJ_ROWS) * ADJ_ROWS, ADJ_ROWS), ADJ_ROWS)
            adj[k, rows, :] = jnp.dot(sym[k, rows, :], field[:, cols], preferred_element_type=F32)
            return 0
        lax.fori_loop(0, 2048 // ADJ_ROWS, block, 0)

        def group(g, acc):
            rows = pl.ds(pl.multiple_of(g * GROUP, GROUP), GROUP)

            def load(start):
                return field[rows, pl.ds(pl.multiple_of(start, 128), NY)].astype(F32)

            new = list(acc)
            n = 0
            u = load(col + r0 * NY)
            for r in (r0, r0 + 1):
                ahead = load(col + (r + 1) * NY)
                near = (ahead * row_keep if r == ROWS - 1 else ahead) + pltpu.roll(u, NY - 1, 1) * lane_keep[:1]
                if odd:
                    near = near + load(ZCOL + pair * OWN + r * NY) * z_keep
                    above = load(col - SLAB + r * NY)
                for k in range(2):
                    v = adj[k, rows, pl.ds((r - r0) * NY, NY)]
                    for other_u in ((u, near, above) if odd else (u, near)):
                        t = other_u * v
                        new[n] = new[n] + jnp.sum(t.reshape(GROUP // 8, 8, NY), axis=0)
                        n += 1
                u = ahead
            return tuple(new)

        per = 3 if odd else 2
        acc = lax.fori_loop(0, ELECTRODES // GROUP, group, tuple(jnp.zeros((8, NY), F32) for _ in range(4 * per)))
        n = 0
        for r in (r0, r0 + 1):
            for k in range(2):
                row = k * ROWS + r
                total = [jnp.sum(acc[n + t], axis=0, keepdims=True) for t in range(per)]
                n += per
                q = 0.5 * total[0]
                q_own[slot, row:row + 1, :] = q
                if r > 0:
                    q_ahead[slot, row - 1:row, :] = q
                else:
                    q_row[pl.ds(slot * 2 + k, 1), :] = q
                cross[slot, row:row + 1, :] = total[1]
                if odd:
                    cross[slot - 1, row:row + 1, :] += total[2]

    def q_depth_copy(pair):
        j, target = halo_target(pair)
        return pltpu.make_async_remote_copy(
            src_ref=q_own.at[pair * 2], dst_ref=q_depth_in.at[j], send_sem=qs_sem.at[pair], recv_sem=qr_sem.at[j],
            device_id=target, device_id_type=MESH)

    def q_depth_arrival(j):
        return pltpu.make_async_remote_copy(
            src_ref=q_own.at[0], dst_ref=q_depth_in.at[j], send_sem=qs_sem.at[j], recv_sem=qr_sem.at[j],
            device_id=device_of(x, y, z, 1 - c), device_id_type=MESH)

    def q_row_copy():
        return pltpu.make_async_remote_copy(
            src_ref=q_row, dst_ref=q_row_in, send_sem=qs_sem.at[2], recv_sem=qr_sem.at[2],
            device_id=row_device(lax.rem(row_block + 15, 16)), device_id_type=MESH)

    near_pair = 1 - xl
    far_pair = xl
    work(near_pair, 0, 0)
    work(near_pair, 0, 2)
    pass_on(1, 2, 0)
    work(far_pair, 0, 0)
    work(far_pair, 0, 2)
    pass_on(1, 2, 1)
    for j in range(2):
        q_depth_copy(j).start()
    for j in range(2):
        for half in range(2):
            halo_arrival(j, half).wait_recv()
    y_wait(1, 1)
    y_wait(1, 3)
    work(near_pair, 1, 0)
    work(near_pair, 1, 2)
    y_wait(1, 0)
    y_wait(1, 2, (0, 1))
    work(far_pair, 1, 0)
    q_row_copy().start()
    y_wait(1, 2, (2,))
    work(far_pair, 1, 2)
    for j in range(2):
        q_depth_arrival(j).wait_recv()
    q_row_copy().wait_recv()

    edge_lane = lane_keep
    sub_row = lax.rem(lax.broadcasted_iota(jnp.int32, (8, NY), 0), ROWS)
    x_valid = jnp.where(sub_row == ROWS - 1, row_keep, 1.0)
    for slot in range(4):
        for k in range(2):
            row = k * ROWS + ROWS - 1
            q_ahead[slot, row:row + 1, :] = q_row_in[slot * 2 + k:slot * 2 + k + 1, :] * row_keep
        z_valid = depth_keep if slot == 3 else 1.0
        q = q_own[slot]
        q_below = q_own[slot + 1] if slot % 2 == 0 else q_depth_in[slot // 2] * z_valid
        sens[slot] = (x_valid + edge_lane + z_valid) * q + q_ahead[slot] + pltpu.roll(q, NY - 1, 1) * edge_lane + q_below - cross[slot]

    def hand_over(j):
        return pltpu.make_async_remote_copy(
            src_ref=sens.at[pl.ds(2 * j, 2)], dst_ref=other.at[lax.rem(y, 2)], send_sem=ps_sem.at[j], recv_sem=pr_sem.at[lax.rem(y, 2)],
            device_id=owner(j), device_id_type=MESH)

    def hand_over_arrival(h):
        return pltpu.make_async_remote_copy(
            src_ref=sens.at[pl.ds(0, 2)], dst_ref=other.at[h], send_sem=ps_sem.at[h], recv_sem=pr_sem.at[h],
            device_id=holder(h), device_id_type=MESH)

    for j in range(2):
        @pl.when(jnp.logical_not(owner_is_me(j)))
        def _():
            hand_over(j).start()

        @pl.when(owner_is_me(j))
        def _():
            other[lax.rem(y, 2)] = sens[pl.ds(2 * j, 2)]
    rate = -(cond[...] * inside[...].astype(F32))
    for p in range(2):
        for r in range(8):
            cond_t[p, r:r + 1, :] = rate[p:p + 1, r * NY:(r + 1) * NY]
    for h in range(2):
        @pl.when(jnp.logical_not(holder_is_me(h)))
        def _():
            hand_over_arrival(h).wait_recv()
    first = other[0]
    second = other[1]
    gradient = [[cond_t[p] * jnp.concatenate([first[p, k * ROWS:(k + 1) * ROWS], second[p, k * ROWS:(k + 1) * ROWS]], axis=0)
                 for p in range(2)] for k in range(2)]
    depth0 = (s * 2).astype(F32)
    weight0 = 1.0 + 2.0 * depth0 / 32.0
    weight1 = 1.0 + 2.0 * (depth0 + 1.0) / 32.0
    run0 = [weight0 * gradient[k][0] * gradient[k][0] for k in range(2)]
    run1 = [run0[k] + weight1 * gradient[k][1] * gradient[k][1] for k in range(2)]
    for k in range(2):
        totals[16, k] = run1[k]

    def total_copy(i):
        return pltpu.make_async_remote_copy(
            src_ref=totals.at[16], dst_ref=totals.at[s], send_sem=ts_sem.at[i], recv_sem=tr_sem.at[s],
            device_id=(e, i), device_id_type=MESH)

    def total_arrival(i):
        return pltpu.make_async_remote_copy(
            src_ref=totals.at[16], dst_ref=totals.at[i], send_sem=ts_sem.at[i], recv_sem=tr_sem.at[i],
            device_id=(e, i), device_id_type=MESH)

    lax.fori_loop(s + 1, 16, lambda i, _: (total_copy(i).start(), 0)[1], 0)

    def add_total(i, before):
        total_arrival(i).wait_recv()
        return before + totals[i]
    prefix = lax.fori_loop(0, s, add_total, jnp.zeros((2, 8, NY), F32))
    for k in range(2):
        for p, run in ((0, run0[k]), (1, run1[k])):
            g = gradient[k][p]
            scaled = g / jnp.sqrt(1.0 + (prefix[k] + run) / (depth0 + (p + 1.0)))
            for r in range(8):
                grad_out[k, p:p + 1, r * NY:(r + 1) * NY] = g[r:r + 1]
                scaled_out[k, p:p + 1, r * NY:(r + 1) * NY] = scaled[r:r + 1]

    lax.fori_loop(s + 1, 16, lambda i, _: (total_copy(i).wait_send(), 0)[1], 0)
    for p in range(2):
        for d in range(4):
            if d > 0:
                for h in range(len(x_parts())):
                    x_copy(p, d, h).wait_send()
            for m in range(len(pieces(p, d))):
                for dy in (1, 3, 2):
                    y_copy(p, d, m, dy).wait_send()
    for j in range(2):
        q_depth_copy(j).wait_send()

        @pl.when(jnp.logical_not(owner_is_me(j)))
        def _():
            hand_over(j).wait_send()
    q_row_copy().wait_send()
    for d in range(4):
        halo_copy(d).wait_send()
    for part in range(2):
        for d in (1, 3, 2):
            w_copy(part, d).wait_send()
        for d in range(4):
            w_across(part, d).wait_send()


def per_device(potentials, measurements, residuals, conductivity, inside):
    vmem = pl.BlockSpec(memory_space=pltpu.VMEM)
    dma = pltpu.SemaphoreType.DMA
    shape = jax.ShapeDtypeStruct((2, 2, 1024), F32)
    tile = (8, NY)
    results = pl.pallas_call(
        kernel_body,
        out_shape=(shape, shape),
        in_specs=[pl.BlockSpec(memory_space=pl.ANY), vmem, vmem, vmem, vmem],
        out_specs=(vmem, vmem),
        scratch_shapes=[
            pltpu.VMEM((2, 128, 8192), F32),
            pltpu.VMEM((2, 128, 8192 + NY), BF),
            pltpu.VMEM((2, 3, 128, XROWS * NY), BF),
            pltpu.VMEM((ELECTRODES, 4 * SLAB + 2 * OWN), BF),
            pltpu.VMEM((2, ELECTRODES, ELECTRODES), BF),
            pltpu.VMEM((2, ELECTRODES, ELECTRODES), BF),
            pltpu.VMEM((2, 2, 256, 256), F32),
            pltpu.VMEM((2, ELECTRODES, 2 * NY), F32),
            pltpu.VMEM((2,) + tile, F32),
            pltpu.VMEM((4,) + tile, F32),
            pltpu.VMEM((4,) + tile, F32),
            pltpu.VMEM((4,) + tile, F32),
            pltpu.VMEM(tile, F32),
            pltpu.VMEM(tile, F32),
            pltpu.VMEM((2,) + tile, F32),
            pltpu.VMEM((4,) + tile, F32),
            pltpu.VMEM((2, 2) + tile, F32),
            pltpu.VMEM((17, 2) + tile, F32),
            dma((2, 4)), dma((2, 4)), dma((2, 4, 2)), dma((2, 4, 2)), dma((2, 4, 3, 4)), dma((2, 4, 3, 4)), dma((4,)), dma((4,)),
            dma((2, 4)), dma((2, 4)), dma((2, 4)), dma((2, 4)), dma((2,)), dma((2,)), dma((16,)), dma((16,)), dma((3,)), dma((3,)),
        ],
        compiler_params=pltpu.CompilerParams(collective_id=0, has_side_effects=True, vmem_limit_bytes=60 << 20),
        name="misfit_gradient",
    )(potentials, measurements.T, residuals, conductivity, inside)

    def hand_out(gradient, scaled, gradient_out, scaled_out):
        gradient_out[...] = gradient[...]
        scaled_out[...] = scaled[...]

    return pl.pallas_call(hand_out, out_shape=(shape, shape), in_specs=[vmem, vmem], out_specs=(vmem, vmem), name="hand_out")(*results)


def solution(mesh):
    return jax.shard_map(
        per_device,
        mesh=mesh,
        in_specs=(P("space", "elec", None), P(), P(), P("space", "elec"), P("space", "elec")),
        out_specs=(P(None, "space", "elec"), P(None, "space", "elec")),
        check_vma=False,
    )
```

```python
import functools

import jax
import jax.numpy as jnp
from jax import lax
from jax.experimental import pallas as pl
from jax.experimental.pallas import tpu as pltpu
from jax.sharding import PartitionSpec as P

ELECTRODES = 1024
NY = 128
ROWS = 4
SLAB = (ROWS + 1) * NY
OWN = ROWS * NY
MESH = pl.DeviceIdType.MESH
BF = jnp.bfloat16
F32 = jnp.float32
QUAD_CHUNK = 2048
XROWS = 4 * ROWS + 1
GROUP = 512
ADJ_ROWS = 1024
ZCOL = 4 * SLAB


def device_of(x, y, z, c):
    return (lax.div(x, 2) * 4 + y, z * 4 + lax.rem(x, 2) * 2 + c)


def kernel_body(pot, quads, resid, cond, inside, grad_out, scaled_out,
                stage, send, mid, field, weights, sym, wacc, adj, cond_t, q_own, q_ahead, cross, q_row, q_row_in, q_depth_in,
                sens, other, totals,
                stage_sem, loc_sem, xs_sem, xr_sem, ys_sem, yr_sem, zs_sem, zr_sem, ws_sem, wr_sem, ds_sem, dr_sem,
                ps_sem, pr_sem, ts_sem, tr_sem, qs_sem, qr_sem):
    e = lax.axis_index("elec")
    s = lax.axis_index("space")
    y = lax.rem(e, 4)
    xh = lax.div(e, 4)
    c = lax.rem(s, 2)
    xl = lax.rem(lax.div(s, 2), 2)
    z = lax.div(s, 4)
    x = xh * 2 + xl
    row_block = x * 4 + y

    cells = pot.shape[2]
    quarter = cells // 4

    def stage_copy(p, q):
        cols = pl.ds(q * quarter, quarter)
        return pltpu.make_async_copy(pot.at[p, :, cols], stage.at[p, :, cols], stage_sem.at[p, q])

    for p in range(2):
        for q in range(4):
            stage_copy(p, q).start()

    def owner(j):
        return device_of(lax.div(x, 2) * 2 + j, 2 * lax.rem(x, 2) + lax.div(y, 2), z, c)

    def owner_is_me(j):
        return jnp.logical_and(xl == j, y == 2 * xl + lax.div(y, 2))

    def holder(h):
        return device_of(2 * xh + lax.div(y, 2), 2 * lax.rem(y, 2) + h, z, c)

    def holder_is_me(h):
        return jnp.logical_and(x == 2 * xh + lax.div(y, 2), y == 2 * lax.rem(y, 2) + h)

    def row_device(b):
        return device_of(lax.div(b, 4), lax.rem(b, 4), z, c)

    bar = pltpu.get_barrier_semaphore()

    def greet(device):
        pl.semaphore_signal(bar, inc=1, device_id=device, device_id_type=MESH)

    for d in range(1, 4):
        greet(device_of(lax.rem(x + d, 4), y, z, c))
        greet(device_of(x, lax.rem(y + d, 4), z, c))
    greet(row_device(lax.rem(row_block + 1, 16)))
    for i in range(1, 16):
        greet((e, lax.rem(s + i, 16)))
    targets = 0
    for j in range(2):
        @pl.when(jnp.logical_not(holder_is_me(j)))
        def _():
            greet(holder(j))
        targets = targets + jnp.where(owner_is_me(j), 0, 1)

    def x_parts():
        return ((0, 64), (64, 64))

    def x_copy(p, d, h):
        tx = lax.rem(x + 4 - d, 4)
        rows = pl.ds(*x_parts()[h])
        return pltpu.make_async_remote_copy(
            src_ref=send.at[p, rows, pl.ds(pl.multiple_of(tx * (4 * OWN), 128), XROWS * NY)], dst_ref=mid.at[p, d - 1, rows],
            send_sem=xs_sem.at[p, d, h], recv_sem=xr_sem.at[p, d, h],
            device_id=device_of(tx, y, z, c), device_id_type=MESH)

    def pieces(p, d):
        if d == 0:
            return ((0, 0, 5),)
        if p == 1 and d == 2:
            return ((0, 0, 5), (1, 0, 3), (1, 3, 2))
        return ((0, 0, 5), (1, 0, 5))

    def slab(p, d, ty, first_e, count, row0, rows):
        xs = lax.rem(x + d, 4)
        es = pl.ds(first_e, count)
        if d == 0:
            src = send.at[p, es, pl.ds(pl.multiple_of((x * 4 + ty) * OWN + row0 * NY, 128), rows * NY)]
        else:
            src = mid.at[p, d - 1, es, pl.ds(pl.multiple_of(ty * OWN + row0 * NY, 128), rows * NY)]
        dst = field.at[pl.ds(pl.multiple_of(lax.div(xs, 2) * 512 + y * 128 + first_e, 64), count),
                       pl.ds(pl.multiple_of((lax.rem(xs, 2) * 2 + p) * SLAB + row0 * NY, 128), rows * NY)]
        return src, dst

    def y_copy(p, d, m, dy):
        ty = lax.rem(y + dy, 4)
        h, row0, rows = pieces(p, d)[m]
        src, dst = slab(p, d, ty, *(x_parts()[h] if d > 0 else (0, 128)), row0, rows)
        return pltpu.make_async_remote_copy(
            src_ref=src, dst_ref=dst, send_sem=ys_sem.at[p, d, m, dy], recv_sem=yr_sem.at[p, d, m, dy],
            device_id=device_of(x, ty, z, c), device_id_type=MESH)

    def local_copy(p, d):
        return pltpu.make_async_copy(*slab(p, d, y, 0, 128, 0, 5), loc_sem.at[p, d])

    def y_start(p, d, h=0):
        for m, piece in enumerate(pieces(p, d)):
            if piece[0] == h:
                for dy in (2, 1, 3):
                    y_copy(p, d, m, dy).start()
        if d == 0 or h == len(x_parts()) - 1:
            local_copy(p, d).start()

    def y_wait(p, d, chosen=None):
        for m in range(len(pieces(p, d))) if chosen is None else chosen:
            for dy in (1, 3, 2):
                y_copy(p, d, m, dy).wait_recv()
        if chosen is None or 0 in chosen:
            local_copy(p, d).wait()

    def pass_on(p, d, h=0):
        x_copy(p, d, h).wait_recv()
        y_start(p, d, h)

    for p in range(2):
        send[p, :, pl.ds(cells, NY)] = jnp.zeros((128, NY), BF)
        for q in range(4):
            stage_copy(p, q).wait()

            def cast(i, _):
                rows = pl.ds(pl.multiple_of(i * 16, 16), 16)
                cols = pl.ds(q * quarter, quarter)
                send[p, rows, cols] = stage[p, rows, cols].astype(BF)
                return 0
            lax.fori_loop(0, 8, cast, 0, unroll=8)
        if p == 0:
            pl.semaphore_wait(bar, 22 + targets)
        for d in (1, 3, 2):
            for h in range(len(x_parts())):
                x_copy(p, d, h).start()
        y_start(p, 0)

    quarter_f = 256
    half_e = 512
    def one_hot(plus, minus, base, count):
        parts = []
        for b in range(0, count, 256):
            ids = lax.broadcasted_iota(jnp.int32, (256, QUAD_CHUNK), 0).astype(F32).astype(BF)
            hit = (plus - (base + b)).astype(F32).astype(BF) == ids
            miss = (minus - (base + b)).astype(F32).astype(BF) == ids
            one = jnp.ones((), BF)
            parts.append(jnp.where(hit, one, jnp.where(miss, -one, jnp.zeros((), BF))))
        return parts[0] if len(parts) == 1 else jnp.concatenate(parts, axis=0)

    def add_quads(part, first, last):
        def step(i, _):
            cols = pl.ds(pl.multiple_of(i * QUAD_CHUNK, QUAD_CHUNK), QUAD_CHUNK)
            left = one_hot(quads[2:3, cols], quads[3:4, cols], z * quarter_f, quarter_f)
            right = one_hot(quads[0:1, cols], quads[1:2, cols], c * half_e + part * 256, 256)
            parts = []
            for k in range(2):
                r = resid[k:k + 1, cols]
                hi = r.astype(BF)
                parts += [left * hi, left * (r - hi.astype(F32)).astype(BF)]
            both = lax.dot_general(jnp.concatenate(parts, axis=0), right, (((1,), (1,)), ((), ())), preferred_element_type=F32)
            for k in range(2):
                wacc[part, k] += both[k * 512:k * 512 + 256] + both[k * 512 + 256:k * 512 + 512]
            return 0
        if first == 0:
            wacc[part] = jnp.zeros(wacc.shape[1:], F32)
        lax.fori_loop(first, last, step, 0)

    def block_of(part, zz, cc):
        return weights.at[:, pl.ds(pl.multiple_of(zz * quarter_f, quarter_f), quarter_f),
                          pl.ds(pl.multiple_of(cc * half_e + part * 256, 256), 256)]

    def w_copy(part, d):
        zz = lax.rem(z + 3, 4) if d == 2 else z
        step = 3 if d == 3 else 1
        return pltpu.make_async_remote_copy(
            src_ref=block_of(part, zz, c), dst_ref=block_of(part, zz, c), send_sem=ws_sem.at[part, d], recv_sem=wr_sem.at[part, d],
            device_id=device_of(x, y, lax.rem(z + step, 4), c), device_id_type=MESH)

    def w_across(part, d):
        zz = lax.rem(z + 4 - d, 4)
        return pltpu.make_async_remote_copy(
            src_ref=block_of(part, zz, c), dst_ref=block_of(part, zz, c), send_sem=ds_sem.at[part, d], recv_sem=dr_sem.at[part, d],
            device_id=device_of(x, y, z, 1 - c), device_id_type=MESH)

    def w_share(part):
        weights[:, pl.ds(pl.multiple_of(z * quarter_f, quarter_f), quarter_f),
                pl.ds(pl.multiple_of(c * half_e + part * 256, 256), 256)] = wacc[part].astype(BF)
        w_copy(part, 1).start()
        w_copy(part, 3).start()
        w_across(part, 0).start()

    def w_forward(part):
        w_copy(part, 1).wait_recv()
        w_copy(part, 2).start()
        w_across(part, 1).start()
        w_copy(part, 3).wait_recv()
        w_across(part, 3).start()

    def w_last(part):
        w_copy(part, 2).wait_recv()
        w_across(part, 2).start()

    chunks = quads.shape[1] // QUAD_CHUNK
    def halo_target(pair):
        down = jnp.logical_and(c == 0, pair == 0)
        j = jnp.where(c == 0, 1 - pair, pair)
        return j, device_of(x, y, jnp.where(down, lax.rem(z + 3, 4), z), 1 - c)

    def halo_copy(d):
        xs = lax.rem(x + d, 4)
        pair = lax.rem(xs, 2)
        half = lax.div(xs, 2)
        j, target = halo_target(pair)
        rows = pl.ds(pl.multiple_of(half * 512, 512), 512)
        return pltpu.make_async_remote_copy(
            src_ref=field.at[rows, pl.ds(pl.multiple_of(pair * (2 * SLAB), 128), OWN)],
            dst_ref=field.at[rows, pl.ds(pl.multiple_of(ZCOL + j * OWN, 128), OWN)],
            send_sem=zs_sem.at[d], recv_sem=zr_sem.at[j * 2 + half], device_id=target, device_id_type=MESH)

    def halo_arrival(j, half):
        return pltpu.make_async_remote_copy(
            src_ref=field.at[pl.ds(0, 512), pl.ds(0, OWN)], dst_ref=field.at[pl.ds(half * 512, 512), pl.ds(ZCOL + j * OWN, OWN)],
            send_sem=zs_sem.at[0], recv_sem=zr_sem.at[j * 2 + half], device_id=device_of(x, y, z, 1 - c), device_id_type=MESH)

    def first_planes(d):
        y_wait(0, d)
        halo_copy(d).start()

    def near_on(p, h):
        pass_on(p, 1, h)
        pass_on(p, 3, h)

    eighth = chunks // 8
    add_quads(0, 0, 5 * eighth)
    near_on(0, 0)
    add_quads(0, 5 * eighth, chunks)
    w_share(0)
    add_quads(1, 0, 2 * eighth)
    near_on(0, 1)
    add_quads(1, 2 * eighth, 5 * eighth)
    w_forward(0)
    add_quads(1, 5 * eighth, 7 * eighth)
    pass_on(0, 2, 0)
    add_quads(1, 7 * eighth, chunks)
    w_share(1)
    w_last(0)
    pass_on(0, 2, 1)
    w_forward(1)
    first_planes(0)
    first_planes(1)
    first_planes(3)
    near_on(1, 0)
    w_last(1)
    for part in range(2):
        for d in range(4):
            w_across(part, d).wait_recv()

    def symmetrize(i, _):
        k = lax.div(i, 16)
        rows = pl.ds(pl.multiple_of(lax.rem(lax.div(i, 4), 4) * 256, 256), 256)
        cols = pl.ds(pl.multiple_of(lax.rem(i, 4) * 256, 256), 256)
        sym[k, rows, cols] = (weights[k, rows, cols].astype(F32) + weights[k, cols, rows].T.astype(F32)).astype(BF)
        return 0
    lax.fori_loop(0, 16, symmetrize, 0, unroll=4)
    near_on(1, 1)
    lax.fori_loop(16, 32, symmetrize, 0, unroll=4)
    first_planes(2)

    lane_keep = (lax.broadcasted_iota(jnp.int32, (8, NY), 1) < NY - 1).astype(F32)
    row_keep = (row_block < 15).astype(F32)
    depth_keep = jnp.logical_or(c == 0, z < 3).astype(F32)

    def work(pair, p, r0):
        slot = pair * 2 + p
        col = slot * SLAB
        odd = p == 1
        cols = pl.ds(pl.multiple_of(col + r0 * NY, 128), 2 * NY)
        z_keep = jnp.where(pair == 1, depth_keep, 1.0)

        def block(i, _):
            k = lax.div(i, 1024 // ADJ_ROWS)
            rows = pl.ds(pl.multiple_of(lax.rem(i, 1024 // ADJ_ROWS) * ADJ_ROWS, ADJ_ROWS), ADJ_ROWS)
            adj[k, rows, :] = jnp.dot(sym[k, rows, :], field[:, cols], preferred_element_type=F32)
            return 0
        lax.fori_loop(0, 2048 // ADJ_ROWS, block, 0)

        def group(g, acc):
            rows = pl.ds(pl.multiple_of(g * GROUP, GROUP), GROUP)

            def load(start):
                return field[rows, pl.ds(pl.multiple_of(start, 128), NY)].astype(F32)

            new = list(acc)
            n = 0
            u = load(col + r0 * NY)
            for r in (r0, r0 + 1):
                ahead = load(col + (r + 1) * NY)
                near = (ahead * row_keep if r == ROWS - 1 else ahead) + pltpu.roll(u, NY - 1, 1) * lane_keep[:1]
                if odd:
                    near = near + load(ZCOL + pair * OWN + r * NY) * z_keep
                    above = load(col - SLAB + r * NY)
                for k in range(2):
                    v = adj[k, rows, pl.ds((r - r0) * NY, NY)]
                    for other_u in ((u, near, above) if odd else (u, near)):
                        t = other_u * v
                        new[n] = new[n] + jnp.sum(t.reshape(GROUP // 8, 8, NY), axis=0)
                        n += 1
                u = ahead
            return tuple(new)

        per = 3 if odd else 2
        acc = lax.fori_loop(0, ELECTRODES // GROUP, group, tuple(jnp.zeros((8, NY), F32) for _ in range(4 * per)))
        n = 0
        for r in (r0, r0 + 1):
            for k in range(2):
                row = k * ROWS + r
                total = [jnp.sum(acc[n + t], axis=0, keepdims=True) for t in range(per)]
                n += per
                q = 0.5 * total[0]
                q_own[slot, row:row + 1, :] = q
                if r > 0:
                    q_ahead[slot, row - 1:row, :] = q
                else:
                    q_row[pl.ds(slot * 2 + k, 1), :] = q
                cross[slot, row:row + 1, :] = total[1]
                if odd:
                    cross[slot - 1, row:row + 1, :] += total[2]

    def q_depth_copy(pair):
        j, target = halo_target(pair)
        return pltpu.make_async_remote_copy(
            src_ref=q_own.at[pair * 2], dst_ref=q_depth_in.at[j], send_sem=qs_sem.at[pair], recv_sem=qr_sem.at[j],
            device_id=target, device_id_type=MESH)

    def q_depth_arrival(j):
        return pltpu.make_async_remote_copy(
            src_ref=q_own.at[0], dst_ref=q_depth_in.at[j], send_sem=qs_sem.at[j], recv_sem=qr_sem.at[j],
            device_id=device_of(x, y, z, 1 - c), device_id_type=MESH)

    def q_row_copy():
        return pltpu.make_async_remote_copy(
            src_ref=q_row, dst_ref=q_row_in, send_sem=qs_sem.at[2], recv_sem=qr_sem.at[2],
            device_id=row_device(lax.rem(row_block + 15, 16)), device_id_type=MESH)

    near_pair = 1 - xl
    far_pair = xl
    work(near_pair, 0, 0)
    work(near_pair, 0, 2)
    pass_on(1, 2, 0)
    work(far_pair, 0, 0)
    work(far_pair, 0, 2)
    pass_on(1, 2, 1)
    for j in range(2):
        q_depth_copy(j).start()
    for j in range(2):
        for half in range(2):
            halo_arrival(j, half).wait_recv()
    y_wait(1, 1)
    y_wait(1, 3)
    work(near_pair, 1, 0)
    work(near_pair, 1, 2)
    y_wait(1, 0)
    y_wait(1, 2, (0, 1))
    work(far_pair, 1, 0)
    q_row_copy().start()
    y_wait(1, 2, (2,))
    work(far_pair, 1, 2)
    for j in range(2):
        q_depth_arrival(j).wait_recv()
    q_row_copy().wait_recv()

    edge_lane = lane_keep
    sub_row = lax.rem(lax.broadcasted_iota(jnp.int32, (8, NY), 0), ROWS)
    x_valid = jnp.where(sub_row == ROWS - 1, row_keep, 1.0)
    for slot in range(4):
        for k in range(2):
            row = k * ROWS + ROWS - 1
            q_ahead[slot, row:row + 1, :] = q_row_in[slot * 2 + k:slot * 2 + k + 1, :] * row_keep
        z_valid = depth_keep if slot == 3 else 1.0
        q = q_own[slot]
        q_below = q_own[slot + 1] if slot % 2 == 0 else q_depth_in[slot // 2] * z_valid
        sens[slot] = (x_valid + edge_lane + z_valid) * q + q_ahead[slot] + pltpu.roll(q, NY - 1, 1) * edge_lane + q_below - cross[slot]

    def hand_over(j):
        return pltpu.make_async_remote_copy(
            src_ref=sens.at[pl.ds(2 * j, 2)], dst_ref=other.at[lax.rem(y, 2)], send_sem=ps_sem.at[j], recv_sem=pr_sem.at[lax.rem(y, 2)],
            device_id=owner(j), device_id_type=MESH)

    def hand_over_arrival(h):
        return pltpu.make_async_remote_copy(
            src_ref=sens.at[pl.ds(0, 2)], dst_ref=other.at[h], send_sem=ps_sem.at[h], recv_sem=pr_sem.at[h],
            device_id=holder(h), device_id_type=MESH)

    for j in range(2):
        @pl.when(jnp.logical_not(owner_is_me(j)))
        def _():
            hand_over(j).start()

        @pl.when(owner_is_me(j))
        def _():
            other[lax.rem(y, 2)] = sens[pl.ds(2 * j, 2)]
    rate = -(cond[...] * inside[...].astype(F32))
    for p in range(2):
        for r in range(8):
            cond_t[p, r:r + 1, :] = rate[p:p + 1, r * NY:(r + 1) * NY]
    for h in range(2):
        @pl.when(jnp.logical_not(holder_is_me(h)))
        def _():
            hand_over_arrival(h).wait_recv()
    first = other[0]
    second = other[1]
    gradient = [[cond_t[p] * jnp.concatenate([first[p, k * ROWS:(k + 1) * ROWS], second[p, k * ROWS:(k + 1) * ROWS]], axis=0)
                 for p in range(2)] for k in range(2)]
    depth0 = (s * 2).astype(F32)
    weight0 = 1.0 + 2.0 * depth0 / 32.0
    weight1 = 1.0 + 2.0 * (depth0 + 1.0) / 32.0
    run0 = [weight0 * gradient[k][0] * gradient[k][0] for k in range(2)]
    run1 = [run0[k] + weight1 * gradient[k][1] * gradient[k][1] for k in range(2)]
    for k in range(2):
        totals[16, k] = run1[k]

    def total_copy(i):
        return pltpu.make_async_remote_copy(
            src_ref=totals.at[16], dst_ref=totals.at[s], send_sem=ts_sem.at[i], recv_sem=tr_sem.at[s],
            device_id=(e, i), device_id_type=MESH)

    def total_arrival(i):
        return pltpu.make_async_remote_copy(
            src_ref=totals.at[16], dst_ref=totals.at[i], send_sem=ts_sem.at[i], recv_sem=tr_sem.at[i],
            device_id=(e, i), device_id_type=MESH)

    lax.fori_loop(s + 1, 16, lambda i, _: (total_copy(i).start(), 0)[1], 0)

    def add_total(i, before):
        total_arrival(i).wait_recv()
        return before + totals[i]
    prefix = lax.fori_loop(0, s, add_total, jnp.zeros((2, 8, NY), F32))
    for k in range(2):
        for p, run in ((0, run0[k]), (1, run1[k])):
            g = gradient[k][p]
            scaled = g / jnp.sqrt(1.0 + (prefix[k] + run) / (depth0 + (p + 1.0)))
            for r in range(8):
                grad_out[k, p:p + 1, r * NY:(r + 1) * NY] = g[r:r + 1]
                scaled_out[k, p:p + 1, r * NY:(r + 1) * NY] = scaled[r:r + 1]

    lax.fori_loop(s + 1, 16, lambda i, _: (total_copy(i).wait_send(), 0)[1], 0)
    for p in range(2):
        for d in range(4):
            if d > 0:
                for h in range(len(x_parts())):
                    x_copy(p, d, h).wait_send()
            for m in range(len(pieces(p, d))):
                for dy in (1, 3, 2):
                    y_copy(p, d, m, dy).wait_send()
    for j in range(2):
        q_depth_copy(j).wait_send()

        @pl.when(jnp.logical_not(owner_is_me(j)))
        def _():
            hand_over(j).wait_send()
    q_row_copy().wait_send()
    for d in range(4):
        halo_copy(d).wait_send()
    for part in range(2):
        for d in (1, 3, 2):
            w_copy(part, d).wait_send()
        for d in range(4):
            w_across(part, d).wait_send()


def per_device(potentials, measurements, residuals, conductivity, inside):
    vmem = pl.BlockSpec(memory_space=pltpu.VMEM)
    dma = pltpu.SemaphoreType.DMA
    shape = jax.ShapeDtypeStruct((2, 2, 1024), F32)
    tile = (8, NY)
    results = pl.pallas_call(
        kernel_body,
        out_shape=(shape, shape),
        in_specs=[pl.BlockSpec(memory_space=pl.ANY), vmem, vmem, vmem, vmem],
        out_specs=(vmem, vmem),
        scratch_shapes=[
            pltpu.VMEM((2, 128, 8192), F32),
            pltpu.VMEM((2, 128, 8192 + NY), BF),
            pltpu.VMEM((2, 3, 128, XROWS * NY), BF),
            pltpu.VMEM((ELECTRODES, 4 * SLAB + 2 * OWN), BF),
            pltpu.VMEM((2, ELECTRODES, ELECTRODES), BF),
            pltpu.VMEM((2, ELECTRODES, ELECTRODES), BF),
            pltpu.VMEM((2, 2, 256, 256), F32),
            pltpu.VMEM((2, ELECTRODES, 2 * NY), F32),
            pltpu.VMEM((2,) + tile, F32),
            pltpu.VMEM((4,) + tile, F32),
            pltpu.VMEM((4,) + tile, F32),
            pltpu.VMEM((4,) + tile, F32),
            pltpu.VMEM(tile, F32),
            pltpu.VMEM(tile, F32),
            pltpu.VMEM((2,) + tile, F32),
            pltpu.VMEM((4,) + tile, F32),
            pltpu.VMEM((2, 2) + tile, F32),
            pltpu.VMEM((17, 2) + tile, F32),
            dma((2, 4)), dma((2, 4)), dma((2, 4, 2)), dma((2, 4, 2)), dma((2, 4, 3, 4)), dma((2, 4, 3, 4)), dma((4,)), dma((4,)),
            dma((2, 4)), dma((2, 4)), dma((2, 4)), dma((2, 4)), dma((2,)), dma((2,)), dma((16,)), dma((16,)), dma((3,)), dma((3,)),
        ],
        compiler_params=pltpu.CompilerParams(collective_id=0, has_side_effects=True, vmem_limit_bytes=60 << 20),
        name="misfit_gradient",
    )(potentials, measurements.T, residuals, conductivity, inside)

    def hand_out(gradient, scaled, gradient_out, scaled_out):
        gradient_out[...] = gradient[...]
        scaled_out[...] = scaled[...]

    return pl.pallas_call(hand_out, out_shape=(shape, shape), in_specs=[vmem, vmem], out_specs=(vmem, vmem), name="hand_out")(*results)


def solution(mesh):
    return jax.shard_map(
        per_device,
        mesh=mesh,
        in_specs=(P("space", "elec", None), P(), P(), P("space", "elec"), P("space", "elec")),
        out_specs=(P(None, "space", "elec"), P(None, "space", "elec")),
        check_vma=False,
    )
```
